512 devices in a mesh: mp: 8 (over z_hi, core), ctx: 64 (over z_lo, x, y).
Axes of the slice: x: 4, y: 8, z: 8 (z_hi: 4, z_lo: 2; z = z_hi * 2 + z_lo), core: 2. Of those that a mesh axis runs over, the one named last changes fastest.
Arguments:
- x_in: bfloat16 [16384, 8192], P('ctx', 'mp'), may hold values from -6 to 6
- z_gate: bfloat16 [16384, 8192], P('ctx', 'mp'), may hold values from -6 to 6
- dt_raw: bfloat16 [16384, 8192], P('ctx', 'mp'), may hold values from -6 to 6
- b_proj: bfloat16 [16384, 16], P('ctx'), may hold values from -0.6 to 0.6
- c_proj: bfloat16 [16384, 16], P('ctx'), may hold values from -1.796875 to 1.796875
- conv_weight: float32 [4, 8192], P(None, 'mp'), may hold values from -3 to 3
- conv_bias: float32 [8192], P('mp'), may hold values from -3 to 3
- a_log: float32 [16, 8192], P(None, 'mp'), may hold values from -11.4 to -2.8, as said below
- d_skip: float32 [8192], P('mp'), may hold values from 0.5 to 1.5
Outputs:
- mamba_out: bfloat16 [16384, 8192], P('ctx', 'mp')
The draws below stay inside these ranges and needn't reach their ends.
Inputs may be any that keep to these rules, and one draw needn't show every extreme that they name: a_log holds logarithms of positive decay rates.
All inputs are finite; a program needn't handle non-finite values.
Results may differ from the reference program's by a relative error of at most 0.0014.
Values may be sent and summed in bfloat16 or wider, within the bound.
A program may use at most 64 MiB of HBM per device.

```python
import math
import jax
import jax.numpy as jnp
from jax import lax

INNER = 8192
STATE = 16
CONV = 4
TOKENS = 16384


def draw_a_log(key, part):
    own_key = jax.random.fold_in(key, 5)
    pick_key, slow_key, fast_key = jax.random.split(own_key, 3)
    slow = jax.random.uniform(slow_key, (STATE, INNER), jnp.float32, math.log(0.3 / TOKENS), math.log(2.5 / TOKENS))
    fast = jax.random.uniform(fast_key, (STATE, INNER), jnp.float32, math.log(0.02), math.log(0.06))
    chooser = jax.random.uniform(pick_key, (STATE, INNER), jnp.float32) < 0.5
    return jnp.where(chooser, fast, slow).astype(jnp.float32)


def draw_dt_raw(key, part):
    own_key = jax.random.fold_in(key, 7)
    noise_key = jax.random.fold_in(own_key, 2)
    values = jax.random.truncated_normal(noise_key, -6.0, 6.0, (TOKENS, INNER), jnp.float32)
    return jnp.clip(values, -6.0, 6.0).astype(jnp.bfloat16)


def draw_x_in(key, part):
    own_key = jax.random.fold_in(key, 9)
    noise_key = jax.random.fold_in(own_key, 1)
    values = jax.random.truncated_normal(noise_key, -6.0, 6.0, (TOKENS, INNER), jnp.float32)
    return jnp.clip(values, -6.0, 6.0).astype(jnp.bfloat16)


def draw_b_proj(key, part):
    own_key = jax.random.fold_in(key, 11)
    noise_key = jax.random.fold_in(own_key, 5)
    values = 0.1 * jax.random.truncated_normal(noise_key, -6.0, 6.0, (TOKENS, STATE), jnp.float32)
    return jnp.clip(values, -0.6, 0.6).astype(jnp.bfloat16)


def block_scale(key, shape, pieces, smallest, largest):
    factor_of, own = 1.0, jax.random.fold_in(key, 6)
    for position, blocks in pieces:
        draws = jnp.exp(jax.random.uniform(jax.random.fold_in(own, position), (blocks,), jnp.float32, smallest / len(pieces), largest / len(pieces)))
        factor_of = factor_of * jnp.repeat(draws, shape[position] // blocks).reshape([-1 if axis == position else 1 for axis in range(len(shape))])
    return factor_of


def noise(key, extent, scale, limit, cuts=(), kind=jnp.bfloat16):
    factor_of = block_scale(key, extent, cuts, -0.22, 0.18) if cuts else 1.0
    values = jax.random.normal(key, extent, jnp.float32) * scale * factor_of
    return jnp.minimum(jnp.maximum(values, -limit), limit).astype(kind)


def setup_inputs(seed: int = 0) -> dict:
    key_of = jax.random.split(jax.random.key(seed), 10)
    x_in = draw_x_in(jax.random.fold_in(key_of[9], 71), 0)
    z_gate = noise(key_of[1], (TOKENS, INNER), 1.0, 6.0, ((0, 64), (1, 8)))
    dt_raw = draw_dt_raw(jax.random.fold_in(key_of[9], 71), 0)
    b_proj = draw_b_proj(jax.random.fold_in(key_of[9], 71), 0)
    c_proj = noise(key_of[4], (TOKENS, STATE), 0.3, 1.796875, ((0, 64),))
    conv_weight = noise(key_of[5], (CONV, INNER), CONV ** -0.5, 3.0, ((1, 8),), jnp.float32)
    conv_bias = noise(key_of[6], (INNER,), 0.5, 3.0, ((0, 8),), jnp.float32)
    a_log = draw_a_log(jax.random.fold_in(key_of[9], 71), 0)
    d_skip = jnp.clip(0.5 + 1.0 * jax.random.uniform(key_of[8], (INNER,), jnp.float32) ** block_scale(key_of[8], (INNER,), ((0, 8),), -0.2, 0.2), 0.5, 1.5)
    return dict(x_in=x_in, z_gate=z_gate, dt_raw=dt_raw, b_proj=b_proj, c_proj=c_proj, conv_weight=conv_weight, conv_bias=conv_bias, a_log=a_log, d_skip=d_skip)


def reference(x_in, z_gate, dt_raw, b_proj, c_proj, conv_weight, conv_bias, a_log, d_skip):
    rates = -jnp.exp(a_log)

    def token_step(carried, inputs):
        ssm_state, recent = carried
        x_row, z_row, raw_row, b_row, c_row = inputs
        window = jnp.concatenate([recent, x_row.astype(jnp.float32)[None, :]], 0)
        conv_sum = conv_bias + jnp.sum(conv_weight * window, axis=0)
        inner_act = jax.nn.silu(conv_sum)
        step_size = jax.nn.softplus(raw_row.astype(jnp.float32))
        ssm_state = jnp.exp(step_size[None, :] * rates) * ssm_state + (step_size * inner_act)[None, :] * b_row.astype(jnp.float32)[:, None]
        mixed = jnp.sum(c_row.astype(jnp.float32)[:, None] * ssm_state, axis=0) + d_skip * inner_act
        result = (mixed * jax.nn.silu(z_row.astype(jnp.float32))).astype(jnp.bfloat16)
        return (ssm_state, window[1:]), result

    start = (jnp.zeros((STATE, INNER), jnp.float32), jnp.zeros((CONV - 1, INNER), jnp.float32))
    _, outputs = lax.scan(token_step, start, (x_in, z_gate, dt_raw, b_proj, c_proj))
    return outputs
```

```python
import functools

import jax
import jax.numpy as jnp
from jax import lax
from jax.experimental import pallas as pl
from jax.experimental.pallas import tpu as pltpu
from jax.sharding import PartitionSpec as P

MESH = pl.DeviceIdType.MESH
F32 = jnp.float32
LANES = 128
SUB = 8
LINE = 8
HEAD = 4
LOG2E = 1.4426950408889634
LN2 = 0.6931471805599453
SHARES = ((0, 1, 2, 3, 4, 5), (6, 7, 8, 9, 10, 11), (12, 13, 14, 15))


def tile(index, count=1):
    if isinstance(index, int):
        return pl.ds(index * SUB, count * SUB)
    return pl.ds(pl.multiple_of(index * SUB, SUB), count * SUB)


def splat(ref, index):
    return ref[pl.ds(index, SUB, stride=0), :]


def kernel(lines, x_hbm, z_hbm, dt_hbm, b_hbm, c_hbm, w_hbm, bias_hbm, a_hbm, skip_hbm, out_ref,
           x_in, z_in, dt_in, b_in, c_in, w_in, bias_in, a_in, skip_in,
           x_rows, dt_rows, u_rows, sum_rows, y_rows, gate, b_splat, c_splat, rates, taps, decayed, ends,
           halo, parts_out, parts_in, total_out, total_in, carry, spans, starts_out, starts,
           load_sem, halo_sem, send1, recv1, send2, recv2, send3, recv3):
    tokens, channels = x_in.shape
    states = a_in.shape[0]
    per = states // LINE
    groups = channels // LANES
    me = lax.axis_index("ctx")
    line, place = me // LINE, me % LINE
    count = lines * LINE

    pairs = ((dt_hbm, dt_in), (a_hbm, a_in), (b_hbm, b_in), (x_hbm, x_in), (w_hbm, w_in),
             (bias_hbm, bias_in), (skip_hbm, skip_in), (c_hbm, c_in), (z_hbm, z_in))
    loads = [pltpu.make_async_copy(src, dst, load_sem.at[i]) for i, (src, dst) in enumerate(pairs)]
    for load in loads:
        load.start()
    dt_load, a_load, b_load, x_load, w_load, bias_load, skip_load, c_load, z_load = loads

    def in_line(step):
        return line * LINE + (place + step) % LINE

    barrier = pltpu.get_barrier_semaphore()
    for step in range(1, LINE):
        pl.semaphore_signal(barrier, inc=1, device_id={"ctx": in_line(step)}, device_id_type=MESH)
    for other in range(lines):
        @pl.when(other != line)
        def _():
            pl.semaphore_signal(barrier, inc=1, device_id={"ctx": other * LINE + place}, device_id_type=MESH)

    @pl.when(me > 0)
    def _():
        pl.semaphore_signal(barrier, inc=1, device_id={"ctx": me - 1}, device_id_type=MESH)

    def copy_to(src, dst, send, recv, target):
        return pltpu.make_async_remote_copy(src_ref=src, dst_ref=dst, send_sem=send, recv_sem=recv,
                                            device_id={"ctx": target}, device_id_type=MESH)

    halo_copy = copy_to(x_rows.at[pl.ds((tokens - 3) * SUB, 3 * SUB)], halo, halo_sem.at[0], halo_sem.at[1], me + 1)

    zero = jnp.zeros((SUB, LANES), F32)
    one = jnp.ones((SUB, LANES), F32)

    dt_load.wait()

    def step_sizes(i, _):
        rows = pl.ds(pl.multiple_of(i * 16, 16), 16)
        for j in range(groups):
            raw = dt_in[rows, j * LANES:(j + 1) * LANES].astype(F32)
            dt_rows[pl.ds(i * 16 * SUB + j, 16, stride=SUB), :] = jnp.log2(1.0 + jnp.exp2(raw * LOG2E))
        return 0

    lax.fori_loop(0, tokens // 16, step_sizes, 0)

    a_load.wait()
    for j in range(groups):
        rates[pl.ds(j, states, stride=SUB), :] = -jnp.exp(a_in[:, j * LANES:(j + 1) * LANES])

    def spread(src, dst):
        wide = 2 * LANES
        for n in range(0, states, 2):
            state_of = lax.broadcasted_iota(jnp.int32, (states, wide), 0)
            lane = lax.broadcasted_iota(jnp.int32, (states, wide), 1)
            pick = jnp.where(state_of == n + lane // LANES, 1.0, 0.0).astype(jnp.bfloat16)
            both = lax.dot_general(src[...], pick, (((0,), (0,)), ((), ())), preferred_element_type=F32)
            dst[n * tokens:(n + 1) * tokens, :] = both[:, :LANES]
            dst[(n + 1) * tokens:(n + 2) * tokens, :] = both[:, LANES:]

    b_load.wait()
    spread(b_in, b_splat)

    x_load.wait()

    def lay_out(i, _):
        rows = pl.ds(pl.multiple_of(i * 16, 16), 16)
        for j in range(groups):
            x_rows[pl.ds(i * 16 * SUB + j, 16, stride=SUB), :] = x_in[rows, j * LANES:(j + 1) * LANES].astype(F32)
        return 0

    lax.fori_loop(0, tokens // 16, lay_out, 0)
    w_load.wait()
    bias_load.wait()
    skip_load.wait()
    for j in range(groups):
        taps[pl.ds(j, 4, stride=SUB), :] = 0.5 * w_in[:, j * LANES:(j + 1) * LANES]
    tap = [taps[tile(k), :] for k in range(4)]
    bias = 0.5 * bias_in[...]
    skip = skip_in[...]

    def mix_token(t, window):
        half = bias + tap[0] * window[0] + tap[1] * window[1] + tap[2] * window[2] + tap[3] * window[3]
        inner = half + half * jnp.tanh(half)
        u_rows[tile(t), :] = dt_rows[tile(t), :] * (inner * LN2)
        y_rows[tile(t), :] = skip * inner

    total = zero
    for t in range(HEAD):
        total = total + dt_rows[tile(t), :]
        sum_rows[tile(t), :] = total
    head_total = total

    def mix(i, carried):
        x0, x1, x2, total = carried
        for k in range(4):
            t = HEAD + i * 4 + k
            x3 = x_rows[tile(t), :]
            mix_token(t, (x0, x1, x2, x3))
            total = total + dt_rows[tile(t), :]
            sum_rows[tile(t), :] = total
            x0, x1, x2 = x1, x2, x3
        return x0, x1, x2, total

    window = tuple(x_rows[tile(t), :] for t in range(HEAD - 3, HEAD))
    *_, total = lax.fori_loop(0, (tokens - HEAD) // 4, mix, window + (total,))

    rate = [rates[tile(n), :] for n in range(states)]

    def advance(t, state):
        step = dt_rows[tile(t), :]
        drive = u_rows[tile(t), :]
        return tuple(jnp.exp2(rate[n] * step) * state[n] + drive * splat(b_splat, n * tokens + t) for n in range(states))

    def local_end(first, steps, state):
        def four(i, state):
            for k in range(4):
                state = advance(first + i * 4 + k, state)
            return state
        return lax.fori_loop(0, steps // 4, four, state)

    half_way = tokens // 2
    state = local_end(HEAD, half_way - HEAD, (zero,) * states)

    pl.semaphore_wait(barrier, LINE - 1 + lines - 1 + jnp.where(me < count - 1, 1, 0))

    @pl.when(me < count - 1)
    def _():
        halo_copy.start()

    state = local_end(half_way, tokens - half_way, state)

    @pl.when(me > 0)
    def _():
        halo_copy.wait_recv()

    @pl.when(me == 0)
    def _():
        halo[...] = jnp.zeros((3 * SUB, LANES), F32)

    window = [halo[tile(t), :] for t in range(3)] + [x_rows[tile(t), :] for t in range(HEAD)]
    for t in range(HEAD):
        mix_token(t, window[t:t + 4])
    early = (zero,) * states
    for t in range(HEAD):
        early = advance(t, early)
    rest = total - head_total
    for n in range(states):
        owner, slot = n // per, n % per
        parts_out[tile(owner * (per + 1) + slot), :] = state[n] + jnp.exp2(rate[n] * rest) * early[n]
    for owner in range(LINE):
        parts_out[tile(owner * (per + 1) + per), :] = total

    size = (per + 1) * SUB
    mine = pl.ds(pl.multiple_of(place * size, SUB), size)
    sent = []
    for step in range(1, LINE):
        target = (place + step) % LINE
        theirs = pl.ds(pl.multiple_of(target * size, SUB), size)
        copy = copy_to(parts_out.at[theirs], parts_in.at[mine], send1.at[step], recv1.at[step], line * LINE + target)
        copy.start()
        sent.append(copy)
    parts_in[mine, :] = parts_out[mine, :]

    def read_out(mine_states):
        def four(i, carried):
            states_now, decays = carried
            for k in range(2):
                t = i * 2 + k
                step = dt_rows[tile(t), :]
                drive = u_rows[tile(t), :]
                y = y_rows[tile(t), :]
                states_next, decays_next = [], []
                for m, n in enumerate(mine_states):
                    decay = jnp.exp2(rates[tile(n), :] * step)
                    read = splat(c_splat, n * tokens + t)
                    now = decay * states_now[m] + drive * splat(b_splat, n * tokens + t)
                    since = decay * decays[m]
                    y = y + read * now
                    decayed[tile(n * tokens + t), :] = read * since
                    states_next.append(now)
                    decays_next.append(since)
                y_rows[tile(t), :] = y
                states_now, decays = tuple(states_next), tuple(decays_next)
            return states_now, decays
        size = len(mine_states)
        lax.fori_loop(0, tokens // 2, four, ((zero,) * size, (one,) * size))

    c_load.wait()
    spread(c_in, c_splat)
    read_out(SHARES[0])

    for copy in sent:
        copy.wait_recv()
    own_rate = [rates[tile(place * per + m), :] for m in range(per)]
    ahead = [zero] * per
    span = zero
    for other in range(LINE):
        step = parts_in[tile(other * (per + 1) + per), :]
        for m in range(per):
            starts_out[tile(other * per + m), :] = ahead[m]
            spans[tile(other * per + m), :] = jnp.exp2(own_rate[m] * span)
            ahead[m] = jnp.exp2(own_rate[m] * step) * ahead[m] + parts_in[tile(other * (per + 1) + m), :]
        span = span + step
    for m in range(per):
        total_out[tile(m), :] = ahead[m]
    total_out[tile(per), :] = span

    my_line = pl.ds(pl.multiple_of(line * size, SUB), size)

    def line_copy(step):
        return copy_to(total_out, total_in.at[my_line], send2.at[step], recv2.at[step], (line + step) * LINE + place)

    for step in range(1, lines):
        @pl.when(line + step < lines)
        def _():
            line_copy(step).start()

    z_load.wait()

    def gates(i, _):
        rows = pl.ds(pl.multiple_of(i * 16, 16), 16)
        for j in range(groups):
            half = 0.5 * z_in[rows, j * LANES:(j + 1) * LANES].astype(F32)
            gate[rows, j * LANES:(j + 1) * LANES] = half + half * jnp.tanh(half)
        return 0

    lax.fori_loop(0, tokens // 16, gates, 0)
    read_out(SHARES[1])

    for m in range(per):
        carry[tile(m), :] = zero
    for step in range(lines - 1, 0, -1):
        @pl.when(line >= step)
        def _():
            line_copy(step).wait_recv()
            first = (line - step) * (per + 1)
            step_sum = total_in[tile(first + per), :]
            for m in range(per):
                decay = jnp.exp2(own_rate[m] * step_sum)
                carry[tile(m), :] = decay * carry[tile(m), :] + total_in[tile(first + m), :]

    for other in range(LINE):
        for m in range(per):
            at = tile(other * per + m)
            starts_out[at, :] = starts_out[at, :] + spans[at, :] * carry[tile(m), :]
    returned = []
    mine = tile(place * per, per)
    for step in range(1, LINE):
        target = (place + step) % LINE
        copy = copy_to(starts_out.at[tile(target * per, per)], starts.at[mine], send3.at[step], recv3.at[step],
                       line * LINE + target)
        copy.start()
        returned.append(copy)
    starts[mine, :] = starts_out[mine, :]

    read_out(SHARES[2])

    for copy in returned:
        copy.wait_recv()
    start = [starts[tile(n), :] for n in range(states)]

    def finish(i, _):
        for k in range(16):
            t = i * 16 + k
            terms = [decayed[tile(n * tokens + t), :] * start[n] for n in range(states)] + [y_rows[tile(t), :]]
            while len(terms) > 1:
                terms = [terms[q] + terms[q + 1] if q + 1 < len(terms) else terms[q] for q in range(0, len(terms), 2)]
            y_rows[tile(t), :] = terms[0]
        rows = pl.ds(pl.multiple_of(i * 16, 16), 16)
        for j in range(groups):
            mixed = y_rows[pl.ds(i * 16 * SUB + j, 16, stride=SUB), :]
            at = slice(j * LANES, (j + 1) * LANES)
            out_ref[rows, at] = (mixed * gate[rows, at]).astype(jnp.bfloat16)
        return 0

    lax.fori_loop(0, tokens // 16, finish, 0)

    @pl.when(me < count - 1)
    def _():
        halo_copy.wait_send()

    for copy in sent + returned:
        copy.wait_send()
    for step in range(1, lines):
        @pl.when(line + step < lines)
        def _():
            line_copy(step).wait_send()


def solution(mesh):
    count = mesh.shape["ctx"]
    lines = count // LINE

    def body(x_in, z_gate, dt_raw, b_proj, c_proj, conv_weight, conv_bias, a_log, d_skip):
        tokens, channels = x_in.shape
        states = a_log.shape[0]
        per = states // LINE
        groups = channels // LANES

        def block(*shape, dtype=F32):
            return pltpu.VMEM(shape, dtype)

        def rows(number):
            return block(number * SUB, LANES)

        bf16 = functools.partial(block, dtype=jnp.bfloat16)
        scratch = [
            bf16(tokens, channels), bf16(tokens, channels), bf16(tokens, channels), bf16(states, tokens), bf16(states, tokens),
            block(4, channels), block(SUB, LANES), block(states, channels), block(SUB, LANES),
            rows(tokens), rows(tokens), rows(tokens), rows(tokens), rows(tokens), block(tokens, channels),
            block(states * tokens + SUB, LANES), block(states * tokens + SUB, LANES), rows(states), rows(4),
            rows(states * tokens), rows(states),
            rows(3), rows(LINE * (per + 1)), rows(LINE * (per + 1)), rows(per + 1), rows(lines * (per + 1)), rows(per),
            rows(states), rows(states), rows(states),
            pltpu.SemaphoreType.DMA((9,)), pltpu.SemaphoreType.DMA((2,)),
            pltpu.SemaphoreType.DMA((LINE,)), pltpu.SemaphoreType.DMA((LINE,)),
            pltpu.SemaphoreType.DMA((lines,)), pltpu.SemaphoreType.DMA((lines,)),
            pltpu.SemaphoreType.DMA((LINE,)), pltpu.SemaphoreType.DMA((LINE,)),
        ]
        return pl.pallas_call(
            functools.partial(kernel, lines),
            out_shape=jax.ShapeDtypeStruct((tokens, channels), jnp.bfloat16),
            in_specs=[pl.BlockSpec(memory_space=pltpu.HBM)] * 9,
            out_specs=pl.BlockSpec(memory_space=pltpu.VMEM),
            scratch_shapes=scratch,
            compiler_params=pltpu.CompilerParams(
                collective_id=0, has_side_effects=True, vmem_limit_bytes=48 * 2**20
            ),
        )(x_in, z_gate, dt_raw, b_proj.T, c_proj.T, conv_weight, conv_bias.reshape(groups, LANES), a_log,
          d_skip.reshape(groups, LANES))

    in_specs = (
        P("ctx", "mp"),
        P("ctx", "mp"),
        P("ctx", "mp"),
        P("ctx", None),
        P("ctx", None),
        P(None, "mp"),
        P("mp"),
        P(None, "mp"),
        P("mp"),
    )
    return jax.shard_map(body, mesh=mesh, in_specs=in_specs, out_specs=P("ctx", "mp"), check_vma=False)
```

```python
import functools

import jax
import jax.numpy as jnp
from jax import lax
from jax.experimental import pallas as pl
from jax.experimental.pallas import tpu as pltpu
from jax.sharding import PartitionSpec as P

MESH = pl.DeviceIdType.MESH
F32 = jnp.float32
LANES = 128
SUB = 8
LINE = 8
HEAD = 4
LINE_RANKS = (0, 1, 4, 5, 2, 3, 6, 7)
MIX = 12
SCAN = 28
LOG2E = 1.4426950408889634
LN2 = 0.6931471805599453
SHARES = ((0, 1, 2, 3, 4, 5, 6, 7), (8, 9, 10, 11), (12, 13, 14, 15))


def tile(index, count=1):
    if isinstance(index, int):
        return pl.ds(index * SUB, count * SUB)
    return pl.ds(pl.multiple_of(index * SUB, SUB), count * SUB)


def splat(ref, index):
    return ref[pl.ds(index, SUB, stride=0), :]


def kernel(lines, x_hbm, z_hbm, dt_hbm, b_hbm, c_hbm, w_hbm, bias_hbm, a_hbm, skip_hbm, out_ref,
           x_in, z_in, dt_in, b_in, c_in, w_in, bias_in, a_in, skip_in,
           x_rows, dt_rows, u_rows, y_rows, gate, b_splat, c_splat, rates, taps, decayed,
           halo, parts_out, parts_in, total_out, total_in, carry, spans, starts_out, starts,
           load_sem, place_sem, line_sem, halo_sem, send1, recv1, send2, recv2, send3, recv3):
    tokens, channels = x_in.shape
    states = a_in.shape[0]
    per = states // LINE
    groups = channels // LANES
    me = lax.axis_index("ctx")
    line, place = me // LINE, me % LINE
    count = lines * LINE

    pairs = ((b_hbm, b_in), (a_hbm, a_in), (dt_hbm, dt_in), (x_hbm, x_in), (w_hbm, w_in),
             (bias_hbm, bias_in), (skip_hbm, skip_in), (c_hbm, c_in), (z_hbm, z_in))
    loads = [pltpu.make_async_copy(src, dst, load_sem.at[i]) for i, (src, dst) in enumerate(pairs)]
    for load in loads:
        load.start()
    b_load, a_load, dt_load, x_load, w_load, bias_load, skip_load, c_load, z_load = loads

    mp = lax.axis_index("mp")
    late_line, late_column = (mp == 0) & (line == 0), (mp == 0) & (place == 0)

    def place_rank(at):
        rank = jnp.where(at < LINE // 2, at, LINE + LINE // 2 - 1 - at)
        return jnp.where(late_line, jnp.where(at == 0, LINE - 1, rank - 1), rank)

    def line_rank(at):
        rank = 0
        for other, value in enumerate(LINE_RANKS):
            rank = rank + jnp.where(at == other, value, 0)
        return jnp.where(late_column, jnp.where(at == 0, lines - 1, rank - 1), rank)

    my_place_rank, my_line_rank = place_rank(place), line_rank(line)
    barrier = pltpu.get_barrier_semaphore()

    def signal(semaphore, target):
        pl.semaphore_signal(semaphore, inc=1, device_id={"ctx": target}, device_id_type=MESH)

    for step in range(1, LINE):
        target = (place + step) % LINE

        @pl.when(place_rank(target) > my_place_rank)
        def _():
            signal(barrier, line * LINE + target)
    for other in range(lines):
        @pl.when(line_rank(other) > my_line_rank)
        def _():
            signal(barrier, other * LINE + place)

    @pl.when(jnp.where(place == 0, line > 0, place_rank(place - 1) < my_place_rank))
    def _():
        signal(barrier, me - 1)

    def greet():
        after = jnp.where(place == LINE - 1, me < count - 1, place_rank(place + 1) > my_place_rank)
        pl.semaphore_wait(barrier, my_place_rank + my_line_rank + jnp.where(after, 1, 0))
        for step in range(1, LINE):
            target = (place + step) % LINE

            greeted = (place > 0) if step == LINE - 1 else False

            @pl.when((place_rank(target) < my_place_rank) & jnp.logical_not(greeted))
            def _():
                signal(place_sem.at[LINE - step], line * LINE + target)
        for step in range(1, lines):
            @pl.when((line >= step) & (line_rank(line - step) < my_line_rank))
            def _():
                signal(line_sem.at[step], (line - step) * LINE + place)

    def know_place(step):
        known = (place < LINE - 1) if step == 1 else False

        @pl.when((place_rank((place + step) % LINE) > my_place_rank) & jnp.logical_not(known))
        def _():
            pl.semaphore_wait(place_sem.at[step], 1)

    def know_line(step):
        @pl.when(line_rank(line + step) > my_line_rank)
        def _():
            pl.semaphore_wait(line_sem.at[step], 1)

    def copy_to(src, dst, send, recv, target):
        return pltpu.make_async_remote_copy(src_ref=src, dst_ref=dst, send_sem=send, recv_sem=recv,
                                            device_id={"ctx": target}, device_id_type=MESH)

    halo_copy = copy_to(x_rows.at[pl.ds((tokens - 3) * SUB, 3 * SUB)], halo, halo_sem.at[0], halo_sem.at[1], me + 1)

    zero = jnp.zeros((SUB, LANES), F32)
    one = jnp.ones((SUB, LANES), F32)

    def spread(src, dst, scale=None):
        wide = 2 * LANES
        for n in range(0, states, 2):
            state_of = lax.broadcasted_iota(jnp.int32, (states, wide), 0)
            lane = lax.broadcasted_iota(jnp.int32, (states, wide), 1)
            pick = jnp.where(state_of == n + lane // LANES, 1.0, 0.0).astype(jnp.bfloat16)
            both = lax.dot_general(src[...], pick, (((0,), (0,)), ((), ())), preferred_element_type=F32)
            if scale is not None:
                both = both * scale
            dst[n * tokens:(n + 1) * tokens, :] = both[:, :LANES]
            dst[(n + 1) * tokens:(n + 2) * tokens, :] = both[:, LANES:]

    b_load.wait()
    spread(b_in, b_splat)

    a_load.wait()
    for j in range(groups):
        rates[pl.ds(j, states, stride=SUB), :] = -jnp.exp(a_in[:, j * LANES:(j + 1) * LANES])

    soon = ((place >= LINE // 2) & (place < LINE - 1)) | (late_line & (place == 0))
    pl.when(soon)(greet)
    dt_load.wait()

    def step_sizes(i, _):
        rows = pl.ds(pl.multiple_of(i * 32, 32), 32)
        for j in range(groups):
            raw = dt_in[rows, j * LANES:(j + 1) * LANES].astype(F32)
            dt_rows[pl.ds(i * 32 * SUB + j, 32, stride=SUB), :] = jnp.log2(1.0 + jnp.exp2(raw * LOG2E))
        return 0

    lax.fori_loop(0, tokens // 32, step_sizes, 0)

    x_load.wait()

    def lay_out(i, _):
        rows = pl.ds(pl.multiple_of(i * 32, 32), 32)
        for j in range(groups):
            x_rows[pl.ds(i * 32 * SUB + j, 32, stride=SUB), :] = x_in[rows, j * LANES:(j + 1) * LANES].astype(F32)
        return 0

    lax.fori_loop(0, tokens // 32, lay_out, 0)
    pl.when(jnp.logical_not(soon))(greet)

    @pl.when(me < count - 1)
    def _():
        halo_copy.start()

    w_load.wait()
    bias_load.wait()
    skip_load.wait()
    for j in range(groups):
        taps[pl.ds(j, 4, stride=SUB), :] = 0.5 * w_in[:, j * LANES:(j + 1) * LANES]
    tap = [taps[tile(k), :] for k in range(4)]
    bias = 0.5 * bias_in[...]

    def mix_token(t, window):
        half = bias + tap[0] * window[0] + tap[1] * window[1] + tap[2] * window[2] + tap[3] * window[3]
        inner = half + half * jnp.tanh(half)
        u_rows[tile(t), :] = dt_rows[tile(t), :] * inner
        y_rows[tile(t), :] = inner

    total = zero
    for t in range(HEAD):
        total = total + dt_rows[tile(t), :]
    head_total = total

    def mix(i, carried):
        x0, x1, x2, total = carried
        for k in range(MIX):
            t = HEAD + i * MIX + k
            x3 = x_rows[tile(t), :]
            mix_token(t, (x0, x1, x2, x3))
            total = total + dt_rows[tile(t), :]
            x0, x1, x2 = x1, x2, x3
        return x0, x1, x2, total

    window = tuple(x_rows[tile(t), :] for t in range(HEAD - 3, HEAD))
    *_, total = lax.fori_loop(0, (tokens - HEAD) // MIX, mix, window + (total,))

    def advance(group, t, state):
        step = dt_rows[tile(t), :]
        drive = u_rows[tile(t), :]
        return tuple(jnp.exp2(rates[tile(n), :] * step) * now + drive * splat(b_splat, n * tokens + t)
                     for n, now in zip(group, state))

    def local_end(group):
        def some(i, state):
            for k in range(SCAN):
                state = advance(group, HEAD + i * SCAN + k, state)
            return state
        return lax.fori_loop(0, (tokens - HEAD) // SCAN, some, (zero,) * len(group))

    halves = (range(states // 2), range(states // 2, states))
    state = local_end(halves[0])

    state = state + local_end(halves[1])

    @pl.when(me > 0)
    def _():
        halo_copy.wait_recv()

    @pl.when(me == 0)
    def _():
        halo[...] = jnp.zeros((3 * SUB, LANES), F32)

    window = [halo[tile(t), :] for t in range(3)] + [x_rows[tile(t), :] for t in range(HEAD)]
    for t in range(HEAD):
        mix_token(t, window[t:t + 4])
    early = (zero,) * states
    for t in range(HEAD):
        early = advance(range(states), t, early)
    rest = total - head_total
    for n in range(states):
        owner, slot = n // per, n % per
        parts_out[tile(owner * (per + 1) + slot), :] = state[n] + jnp.exp2(rates[tile(n), :] * rest) * early[n]
    for owner in range(LINE):
        parts_out[tile(owner * (per + 1) + per), :] = total

    size = (per + 1) * SUB
    mine = pl.ds(pl.multiple_of(place * size, SUB), size)
    sent = []
    for step in (1, LINE - 1, 2, LINE - 2, 3, LINE - 3, LINE // 2):
        know_place(step)
        target = (place + step) % LINE
        theirs = pl.ds(pl.multiple_of(target * size, SUB), size)
        copy = copy_to(parts_out.at[theirs], parts_in.at[mine], send1.at[step], recv1.at[step], line * LINE + target)
        copy.start()
        sent.append(copy)
    parts_in[mine, :] = parts_out[mine, :]

    skip = skip_in[...]

    def read_out(mine_states):
        steps = 64 // len(mine_states)

        def some(i, carried):
            states_now, decays = carried
            for k in range(steps):
                t = i * steps + k
                step = dt_rows[tile(t), :]
                drive = u_rows[tile(t), :]
                y = y_rows[tile(t), :]
                if 0 in mine_states:
                    y = skip * y
                states_next, decays_next = [], []
                for m, n in enumerate(mine_states):
                    decay = jnp.exp2(rates[tile(n), :] * step)
                    read = splat(c_splat, n * tokens + t)
                    now = decay * states_now[m] + drive * splat(b_splat, n * tokens + t)
                    since = decay * decays[m]
                    y = y + read * now
                    decayed[tile(t * states + n), :] = read * since
                    states_next.append(now)
                    decays_next.append(since)
                y_rows[tile(t), :] = y
                states_now, decays = tuple(states_next), tuple(decays_next)
            return states_now, decays
        size = len(mine_states)
        lax.fori_loop(0, tokens // steps, some, ((zero,) * size, (one,) * size))

    c_load.wait()
    spread(c_in, c_splat, LN2)
    read_out(SHARES[0])
    z_load.wait()

    def gates(i, _):
        rows = pl.ds(pl.multiple_of(i * 16, 16), 16)
        for j in range(groups):
            half = 0.5 * z_in[rows, j * LANES:(j + 1) * LANES].astype(F32)
            gate[rows, j * LANES:(j + 1) * LANES] = half + half * jnp.tanh(half)
        return 0

    lax.fori_loop(0, tokens // 16, gates, 0)

    for copy in sent:
        copy.wait_recv()
    own_rate = [rates[tile(place * per + m), :] for m in range(per)]
    ahead = [zero] * per
    span = zero
    for other in range(LINE):
        step = parts_in[tile(other * (per + 1) + per), :]
        for m in range(per):
            starts_out[tile(other * per + m), :] = ahead[m]
            spans[tile(other * per + m), :] = jnp.exp2(own_rate[m] * span)
            ahead[m] = jnp.exp2(own_rate[m] * step) * ahead[m] + parts_in[tile(other * (per + 1) + m), :]
        span = span + step
    for m in range(per):
        total_out[tile(m), :] = ahead[m]
    total_out[tile(per), :] = span

    my_line = pl.ds(pl.multiple_of(line * size, SUB), size)

    def line_copy(step):
        return copy_to(total_out, total_in.at[my_line], send2.at[step], recv2.at[step], (line + step) * LINE + place)

    for step in range(1, lines):
        @pl.when(line + step < lines)
        def _():
            know_line(step)
            line_copy(step).start()


    for m in range(per):
        carry[tile(m), :] = zero
    for step in range(lines - 1, 0, -1):
        @pl.when(line >= step)
        def _():
            line_copy(step).wait_recv()
            first = (line - step) * (per + 1)
            step_sum = total_in[tile(first + per), :]
            for m in range(per):
                decay = jnp.exp2(own_rate[m] * step_sum)
                carry[tile(m), :] = decay * carry[tile(m), :] + total_in[tile(first + m), :]

    for other in range(LINE):
        for m in range(per):
            at = tile(other * per + m)
            starts_out[at, :] = starts_out[at, :] + spans[at, :] * carry[tile(m), :]
    returned = []
    mine = tile(place * per, per)
    for step in range(1, LINE):
        target = (place + step) % LINE
        copy = copy_to(starts_out.at[tile(target * per, per)], starts.at[mine], send3.at[step], recv3.at[step],
                       line * LINE + target)
        copy.start()
        returned.append(copy)
    starts[mine, :] = starts_out[mine, :]

    read_out(SHARES[1])
    read_out(SHARES[2])

    def start_terms(owners, t):
        terms = []
        for first, start in owners:
            for m in range(per):
                terms.append(decayed[tile(t * states + first + m), :] * start[m])
        return terms

    def tree(terms):
        while len(terms) > 1:
            terms = [terms[q] + terms[q + 1] if q + 1 < len(terms) else terms[q] for q in range(0, len(terms), 2)]
        return terms[0]

    def arrived(steps):
        owners = []
        for step in steps:
            if step:
                returned[step - 1].wait_recv()
            first = ((place + LINE - step) % LINE) * per
            owners.append((first, [starts[tile(first + m), :] for m in range(per)]))
        return owners

    for steps in ((0, 1, LINE - 1), (2, LINE - 2), (3, LINE - 3)):
        owners = arrived(steps)

        def add(i, _):
            for k in range(16):
                t = i * 16 + k
                y_rows[tile(t), :] = tree(start_terms(owners, t) + [y_rows[tile(t), :]])
            return 0

        lax.fori_loop(0, tokens // 16, add, 0)
    far = arrived((LINE // 2,))

    def finish(i, _):
        for k in range(16):
            t = i * 16 + k
            y_rows[tile(t), :] = tree(start_terms(far, t) + [y_rows[tile(t), :]])
        rows = pl.ds(pl.multiple_of(i * 16, 16), 16)
        for j in range(groups):
            mixed = y_rows[pl.ds(i * 16 * SUB + j, 16, stride=SUB), :]
            at = slice(j * LANES, (j + 1) * LANES)
            out_ref[rows, at] = (mixed * gate[rows, at]).astype(jnp.bfloat16)
        return 0

    lax.fori_loop(0, tokens // 16, finish, 0)

    @pl.when(me < count - 1)
    def _():
        halo_copy.wait_send()

    for copy in sent + returned:
        copy.wait_send()
    for step in range(1, lines):
        @pl.when(line + step < lines)
        def _():
            line_copy(step).wait_send()


def solution(mesh):
    count = mesh.shape["ctx"]
    lines = count // LINE

    def body(x_in, z_gate, dt_raw, b_proj, c_proj, conv_weight, conv_bias, a_log, d_skip):
        tokens, channels = x_in.shape
        states = a_log.shape[0]
        per = states // LINE
        groups = channels // LANES

        def block(*shape, dtype=F32):
            return pltpu.VMEM(shape, dtype)

        def rows(number):
            return block(number * SUB, LANES)

        bf16 = functools.partial(block, dtype=jnp.bfloat16)
        scratch = [
            bf16(tokens, channels), bf16(tokens, channels), bf16(tokens, channels), bf16(states, tokens), bf16(states, tokens),
            block(4, channels), block(SUB, LANES), block(states, channels), block(SUB, LANES),
            rows(tokens), rows(tokens), rows(tokens), rows(tokens), block(tokens, channels),
            block(states * tokens + SUB, LANES), block(states * tokens + SUB, LANES), rows(states), rows(4),
            rows(states * tokens),
            rows(3), rows(LINE * (per + 1)), rows(LINE * (per + 1)), rows(per + 1), rows(lines * (per + 1)), rows(per),
            rows(states), rows(states), rows(states),
            pltpu.SemaphoreType.DMA((9,)), pltpu.SemaphoreType.REGULAR((LINE,)),
            pltpu.SemaphoreType.REGULAR((lines,)), pltpu.SemaphoreType.DMA((2,)),
            pltpu.SemaphoreType.DMA((LINE,)), pltpu.SemaphoreType.DMA((LINE,)),
            pltpu.SemaphoreType.DMA((lines,)), pltpu.SemaphoreType.DMA((lines,)),
            pltpu.SemaphoreType.DMA((LINE,)), pltpu.SemaphoreType.DMA((LINE,)),
        ]
        operands = (x_in, z_gate, dt_raw, b_proj.T, c_proj.T, conv_weight, conv_bias.reshape(groups, LANES), a_log,
                    d_skip.reshape(groups, LANES))
        return pl.pallas_call(
            functools.partial(kernel, lines),
            out_shape=pltpu.VMEM((tokens, channels), jnp.bfloat16),
            in_specs=[pl.BlockSpec(memory_space=pltpu.HBM)] * 9,
            out_specs=pl.BlockSpec(memory_space=pltpu.VMEM),
            scratch_shapes=scratch,
            compiler_params=pltpu.CompilerParams(
                collective_id=0, has_side_effects=True, vmem_limit_bytes=48 * 2**20
            ),
        )(*(pltpu.with_memory_space_constraint(operand, pltpu.HBM) for operand in operands))

    in_specs = (
        P("ctx", "mp"),
        P("ctx", "mp"),
        P("ctx", "mp"),
        P("ctx", None),
        P("ctx", None),
        P(None, "mp"),
        P("mp"),
        P(None, "mp"),
        P("mp"),
    )
    return jax.shard_map(body, mesh=mesh, in_specs=in_specs, out_specs=P("ctx", "mp"), check_vma=False)
```

```python
import functools

import jax
import jax.numpy as jnp
from jax import lax
from jax.experimental import pallas as pl
from jax.experimental.pallas import tpu as pltpu
from jax.sharding import PartitionSpec as P

MESH = pl.DeviceIdType.MESH
F32 = jnp.float32
LANES = 128
SUB = 8
LINE = 8
HEAD = 4
LINE_RANKS = (0, 1, 4, 5, 2, 3, 6, 7)
FAR_FIRST = (4, 3, 5, 2, 6, 1, 7)
BLOCK = 32
SCAN = 42
LOG2E = 1.4426950408889634
LN2 = 0.6931471805599453
SHARES = ((0, 1, 2, 3), (4, 5, 6, 7), (8, 9, 10, 11, 12, 13, 14, 15))


def tile(index, count=1):
    if isinstance(index, int):
        return pl.ds(index * SUB, count * SUB)
    return pl.ds(pl.multiple_of(index * SUB, SUB), count * SUB)


def splat(ref, index):
    return ref[pl.ds(index, SUB, stride=0), :]


def kernel(lines, x_hbm, z_hbm, dt_hbm, b_hbm, c_hbm, w_hbm, bias_hbm, a_hbm, skip_hbm, out_ref,
           x_in, z_in, dt_in, b_in, c_in, w_in, bias_in, a_in, skip_in,
           x_rows, dt_rows, u_rows, y_rows, gate, b_splat, c_splat, rates, taps, decayed,
           halo, parts_out, parts_in, total_out, total_in, carry, spans, starts_out, starts,
           load_sem, dt_sem, x_sem, place_sem, line_sem, halo_sem, send1, recv1, send2, recv2, send3, recv3):
    tokens, channels = x_in.shape
    states = a_in.shape[0]
    per = states // LINE
    groups = channels // LANES
    me = lax.axis_index("ctx")
    line, place = me // LINE, me % LINE
    count = lines * LINE

    pairs = ((b_hbm, b_in), (a_hbm, a_in), (w_hbm, w_in),
             (bias_hbm, bias_in), (skip_hbm, skip_in), (c_hbm, c_in), (z_hbm, z_in))
    loads = [pltpu.make_async_copy(src, dst, load_sem.at[i]) for i, (src, dst) in enumerate(pairs)]
    blocks = tokens // BLOCK

    def chunk(i, src, dst, sem):
        rows = pl.ds(pl.multiple_of(i * BLOCK, BLOCK), BLOCK)
        return pltpu.make_async_copy(src.at[rows], dst.at[rows], sem.at[i])

    def chunks(i):
        return chunk(i, dt_hbm, dt_in, dt_sem), chunk(i, x_hbm, x_in, x_sem)

    for load in loads[:2]:
        load.start()
    for i in range(blocks):
        for load in chunks(i):
            load.start()
    for load in loads[2:]:
        load.start()
    b_load, a_load, w_load, bias_load, skip_load, c_load, z_load = loads

    mp = lax.axis_index("mp")
    late_line, late_column = (mp == 0) & (line == 0), (mp == 0) & (place == 0)

    def place_rank(at):
        rank = jnp.where(at < LINE // 2, at, LINE + LINE // 2 - 1 - at)
        return jnp.where(late_line, jnp.where(at == 0, LINE - 1, rank - 1), rank)

    def line_rank(at):
        rank = 0
        for other, value in enumerate(LINE_RANKS):
            rank = rank + jnp.where(at == other, value, 0)
        return jnp.where(late_column, jnp.where(at == 0, lines - 1, rank - 1), rank)

    my_place_rank, my_line_rank = place_rank(place), line_rank(line)
    barrier = pltpu.get_barrier_semaphore()

    def signal(semaphore, target):
        pl.semaphore_signal(semaphore, inc=1, device_id={"ctx": target}, device_id_type=MESH)

    for step in range(1, LINE):
        target = (place + step) % LINE

        @pl.when(place_rank(target) > my_place_rank)
        def _():
            signal(barrier, line * LINE + target)
    for other in range(lines):
        @pl.when(line_rank(other) > my_line_rank)
        def _():
            signal(barrier, other * LINE + place)

    @pl.when(jnp.where(place == 0, line > 0, place_rank(place - 1) < my_place_rank))
    def _():
        signal(barrier, me - 1)

    def greet():
        after = jnp.where(place == LINE - 1, me < count - 1, place_rank(place + 1) > my_place_rank)
        pl.semaphore_wait(barrier, my_place_rank + my_line_rank + jnp.where(after, 1, 0))
        for step in range(1, LINE):
            target = (place + step) % LINE

            greeted = (place > 0) if step == LINE - 1 else False

            @pl.when((place_rank(target) < my_place_rank) & jnp.logical_not(greeted))
            def _():
                signal(place_sem.at[LINE - step], line * LINE + target)
        for step in range(1, lines):
            @pl.when((line >= step) & (line_rank(line - step) < my_line_rank))
            def _():
                signal(line_sem.at[step], (line - step) * LINE + place)

    def know_place(step):
        known = (place < LINE - 1) if step == 1 else False

        @pl.when((place_rank((place + step) % LINE) > my_place_rank) & jnp.logical_not(known))
        def _():
            pl.semaphore_wait(place_sem.at[step], 1)

    def know_line(step):
        @pl.when(line_rank(line + step) > my_line_rank)
        def _():
            pl.semaphore_wait(line_sem.at[step], 1)

    def copy_to(src, dst, send, recv, target):
        return pltpu.make_async_remote_copy(src_ref=src, dst_ref=dst, send_sem=send, recv_sem=recv,
                                            device_id={"ctx": target}, device_id_type=MESH)

    halo_copy = copy_to(x_rows.at[pl.ds((tokens - 3) * SUB, 3 * SUB)], halo, halo_sem.at[0], halo_sem.at[1], me + 1)

    zero = jnp.zeros((SUB, LANES), F32)
    one = jnp.ones((SUB, LANES), F32)

    def spread(src, dst, scale=None):
        wide = 2 * LANES
        for n in range(0, states, 2):
            state_of = lax.broadcasted_iota(jnp.int32, (states, wide), 0)
            lane = lax.broadcasted_iota(jnp.int32, (states, wide), 1)
            pick = jnp.where(state_of == n + lane // LANES, 1.0, 0.0).astype(jnp.bfloat16)
            both = lax.dot_general(src[...], pick, (((0,), (0,)), ((), ())), preferred_element_type=F32)
            if scale is not None:
                both = both * scale
            dst[n * tokens:(n + 1) * tokens, :] = both[:, :LANES]
            dst[(n + 1) * tokens:(n + 2) * tokens, :] = both[:, LANES:]

    b_load.wait()
    spread(b_in, b_splat)

    a_load.wait()
    for j in range(groups):
        rates[pl.ds(j, states, stride=SUB), :] = -jnp.exp(a_in[:, j * LANES:(j + 1) * LANES])

    soon = ((place >= LINE // 2) & (place < LINE - 1)) | (late_line & (place == 0))
    pl.when(soon)(greet)
    def lay_out(i):
        for load in chunks(i):
            load.wait()
        rows = pl.ds(pl.multiple_of(i * BLOCK, BLOCK), BLOCK)
        for j in range(groups):
            at = pl.ds(i * BLOCK * SUB + j, BLOCK, stride=SUB)
            raw = dt_in[rows, j * LANES:(j + 1) * LANES].astype(F32)
            dt_rows[at, :] = jnp.log2(1.0 + jnp.exp2(raw * LOG2E))
            x_rows[at, :] = x_in[rows, j * LANES:(j + 1) * LANES].astype(F32)

    lay_out(jnp.int32(0))
    w_load.wait()
    bias_load.wait()
    skip_load.wait()
    for j in range(groups):
        taps[pl.ds(j, 4, stride=SUB), :] = 0.5 * w_in[:, j * LANES:(j + 1) * LANES]
    tap = [taps[tile(k), :] for k in range(4)]
    bias = 0.5 * bias_in[...]

    def mix_token(t, window):
        half = bias + tap[0] * window[0] + tap[1] * window[1] + tap[2] * window[2] + tap[3] * window[3]
        inner = half + half * jnp.tanh(half)
        u_rows[tile(t), :] = dt_rows[tile(t), :] * inner
        y_rows[tile(t), :] = inner

    def mix_block(i, carried):
        x0, x1, x2, total = carried
        for k in range(BLOCK):
            t = i * BLOCK + k
            x3 = x_rows[tile(t), :]
            mix_token(t, (x0, x1, x2, x3))
            total = total + dt_rows[tile(t), :]
            x0, x1, x2 = x1, x2, x3
        return x0, x1, x2, total

    def mix(i, carried):
        lay_out(i + 1)
        return mix_block(i, carried)

    carried = lax.fori_loop(0, blocks - 1, mix, (zero,) * 4)
    pl.when(jnp.logical_not(soon))(greet)

    @pl.when(me < count - 1)
    def _():
        halo_copy.start()

    *_, total = mix_block(jnp.int32(blocks - 1), carried)
    head_total = zero
    for t in range(HEAD):
        head_total = head_total + dt_rows[tile(t), :]

    def advance(group, t, state):
        step = dt_rows[tile(t), :]
        drive = u_rows[tile(t), :]
        return tuple(jnp.exp2(rates[tile(n), :] * step) * now + drive * splat(b_splat, n * tokens + t)
                     for n, now in zip(group, state))

    def local_end(group):
        def some(i, state):
            for k in range(SCAN):
                state = advance(group, HEAD + i * SCAN + k, state)
            return state
        return lax.fori_loop(0, (tokens - HEAD) // SCAN, some, (zero,) * len(group))

    halves = (range(states // 2), range(states // 2, states))
    state = local_end(halves[0])

    state = state + local_end(halves[1])

    @pl.when(me > 0)
    def _():
        halo_copy.wait_recv()

    @pl.when(me == 0)
    def _():
        halo[...] = jnp.zeros((3 * SUB, LANES), F32)

    window = [halo[tile(t), :] for t in range(3)] + [x_rows[tile(t), :] for t in range(HEAD)]
    for t in range(HEAD):
        mix_token(t, window[t:t + 4])
    early = (zero,) * states
    for t in range(HEAD):
        early = advance(range(states), t, early)
    rest = total - head_total
    for n in range(states):
        owner, slot = n // per, n % per
        parts_out[tile(owner * (per + 1) + slot), :] = state[n] + jnp.exp2(rates[tile(n), :] * rest) * early[n]
    for owner in range(LINE):
        parts_out[tile(owner * (per + 1) + per), :] = total

    size = (per + 1) * SUB
    mine = pl.ds(pl.multiple_of(place * size, SUB), size)
    sent = []
    for step in FAR_FIRST:
        know_place(step)
        target = (place + step) % LINE
        theirs = pl.ds(pl.multiple_of(target * size, SUB), size)
        copy = copy_to(parts_out.at[theirs], parts_in.at[mine], send1.at[step], recv1.at[step], line * LINE + target)
        copy.start()
        sent.append(copy)
    parts_in[mine, :] = parts_out[mine, :]

    skip = skip_in[...]

    def read_out(mine_states):
        steps = 64 // len(mine_states)

        def some(i, carried):
            states_now, decays = carried
            for k in range(steps):
                t = i * steps + k
                step = dt_rows[tile(t), :]
                drive = u_rows[tile(t), :]
                y = y_rows[tile(t), :]
                if 0 in mine_states:
                    y = skip * y
                states_next, decays_next = [], []
                for m, n in enumerate(mine_states):
                    decay = jnp.exp2(rates[tile(n), :] * step)
                    read = splat(c_splat, n * tokens + t)
                    now = decay * states_now[m] + drive * splat(b_splat, n * tokens + t)
                    since = decay * decays[m]
                    y = y + read * now
                    decayed[tile(t * states + n), :] = read * since
                    states_next.append(now)
                    decays_next.append(since)
                y_rows[tile(t), :] = y
                states_now, decays = tuple(states_next), tuple(decays_next)
            return states_now, decays
        size = len(mine_states)
        lax.fori_loop(0, tokens // steps, some, ((zero,) * size, (one,) * size))

    c_load.wait()
    spread(c_in, c_splat, LN2)
    read_out(SHARES[0])
    for copy in sent:
        copy.wait_recv()
    own_rate = [rates[tile(place * per + m), :] for m in range(per)]
    ahead = [zero] * per
    span = zero
    for other in range(LINE):
        step = parts_in[tile(other * (per + 1) + per), :]
        for m in range(per):
            starts_out[tile(other * per + m), :] = ahead[m]
            spans[tile(other * per + m), :] = jnp.exp2(own_rate[m] * span)
            ahead[m] = jnp.exp2(own_rate[m] * step) * ahead[m] + parts_in[tile(other * (per + 1) + m), :]
        span = span + step
    for m in range(per):
        total_out[tile(m), :] = ahead[m]
    total_out[tile(per), :] = span

    my_line = pl.ds(pl.multiple_of(line * size, SUB), size)

    def line_copy(step):
        return copy_to(total_out, total_in.at[my_line], send2.at[step], recv2.at[step], (line + step) * LINE + place)

    for step in range(1, lines):
        @pl.when(line + step < lines)
        def _():
            know_line(step)
            line_copy(step).start()


    z_load.wait()

    def gates(i, _):
        rows = pl.ds(pl.multiple_of(i * 16, 16), 16)
        for j in range(groups):
            half = 0.5 * z_in[rows, j * LANES:(j + 1) * LANES].astype(F32)
            gate[rows, j * LANES:(j + 1) * LANES] = half + half * jnp.tanh(half)
        return 0

    lax.fori_loop(0, tokens // 16, gates, 0)

    read_out(SHARES[1])

    for m in range(per):
        carry[tile(m), :] = zero
    for step in range(lines - 1, 0, -1):
        @pl.when(line >= step)
        def _():
            line_copy(step).wait_recv()
            first = (line - step) * (per + 1)
            step_sum = total_in[tile(first + per), :]
            for m in range(per):
                decay = jnp.exp2(own_rate[m] * step_sum)
                carry[tile(m), :] = decay * carry[tile(m), :] + total_in[tile(first + m), :]

    for other in range(LINE):
        for m in range(per):
            at = tile(other * per + m)
            starts_out[at, :] = starts_out[at, :] + spans[at, :] * carry[tile(m), :]
    mine = tile(place * per, per)

    def start_copy(step):
        target = (place + step) % LINE
        return copy_to(starts_out.at[tile(target * per, per)], starts.at[mine], send3.at[step], recv3.at[step],
                       line * LINE + target)

    returned = [start_copy(step) for step in range(1, LINE)]
    for target in (0, 1, 2, 3, 7, 6, 5, 4):
        @pl.when(place != target)
        def _():
            start_copy((target + LINE - place) % LINE).start()
    starts[mine, :] = starts_out[mine, :]

    read_out(SHARES[2])

    def start_terms(owners, t):
        terms = []
        for first, start in owners:
            for m in range(per):
                terms.append(decayed[tile(t * states + first + m), :] * start[m])
        return terms

    def tree(terms):
        while len(terms) > 1:
            terms = [terms[q] + terms[q + 1] if q + 1 < len(terms) else terms[q] for q in range(0, len(terms), 2)]
        return terms[0]

    def arrived(steps):
        owners = []
        for step in steps:
            if step:
                returned[step - 1].wait_recv()
            first = ((place + LINE - step) % LINE) * per
            owners.append((first, [starts[tile(first + m), :] for m in range(per)]))
        return owners

    for steps in ((0, 1, LINE - 1), (2, LINE - 2), (3, LINE - 3)):
        owners = arrived(steps)

        def add(i, _):
            for k in range(16):
                t = i * 16 + k
                y_rows[tile(t), :] = tree(start_terms(owners, t) + [y_rows[tile(t), :]])
            return 0

        lax.fori_loop(0, tokens // 16, add, 0)
    far = arrived((LINE // 2,))

    def finish(i, _):
        for k in range(16):
            t = i * 16 + k
            y_rows[tile(t), :] = tree(start_terms(far, t) + [y_rows[tile(t), :]])
        rows = pl.ds(pl.multiple_of(i * 16, 16), 16)
        for j in range(groups):
            mixed = y_rows[pl.ds(i * 16 * SUB + j, 16, stride=SUB), :]
            at = slice(j * LANES, (j + 1) * LANES)
            out_ref[rows, at] = (mixed * gate[rows, at]).astype(jnp.bfloat16)
        return 0

    lax.fori_loop(0, tokens // 16, finish, 0)

    @pl.when(me < count - 1)
    def _():
        halo_copy.wait_send()

    for copy in sent + returned:
        copy.wait_send()
    for step in range(1, lines):
        @pl.when(line + step < lines)
        def _():
            line_copy(step).wait_send()


def solution(mesh):
    count = mesh.shape["ctx"]
    lines = count // LINE

    def body(x_in, z_gate, dt_raw, b_proj, c_proj, conv_weight, conv_bias, a_log, d_skip):
        tokens, channels = x_in.shape
        states = a_log.shape[0]
        per = states // LINE
        groups = channels // LANES

        def block(*shape, dtype=F32):
            return pltpu.VMEM(shape, dtype)

        def rows(number):
            return block(number * SUB, LANES)

        bf16 = functools.partial(block, dtype=jnp.bfloat16)
        scratch = [
            bf16(tokens, channels), bf16(tokens, channels), bf16(tokens, channels), bf16(states, tokens), bf16(states, tokens),
            block(4, channels), block(SUB, LANES), block(states, channels), block(SUB, LANES),
            rows(tokens), rows(tokens), rows(tokens), rows(tokens), block(tokens, channels),
            block(states * tokens + SUB, LANES), block(states * tokens + SUB, LANES), rows(states), rows(4),
            rows(states * tokens),
            rows(3), rows(LINE * (per + 1)), rows(LINE * (per + 1)), rows(per + 1), rows(lines * (per + 1)), rows(per),
            rows(states), rows(states), rows(states),
            pltpu.SemaphoreType.DMA((7,)), pltpu.SemaphoreType.DMA((tokens // BLOCK,)), pltpu.SemaphoreType.DMA((tokens // BLOCK,)), pltpu.SemaphoreType.REGULAR((LINE,)),
            pltpu.SemaphoreType.REGULAR((lines,)), pltpu.SemaphoreType.DMA((2,)),
            pltpu.SemaphoreType.DMA((LINE,)), pltpu.SemaphoreType.DMA((LINE,)),
            pltpu.SemaphoreType.DMA((lines,)), pltpu.SemaphoreType.DMA((lines,)),
            pltpu.SemaphoreType.DMA((LINE,)), pltpu.SemaphoreType.DMA((LINE,)),
        ]
        operands = (x_in, z_gate, dt_raw, b_proj.T, c_proj.T, conv_weight, conv_bias.reshape(groups, LANES), a_log,
                    d_skip.reshape(groups, LANES))
        return pl.pallas_call(
            functools.partial(kernel, lines),
            out_shape=pltpu.VMEM((tokens, channels), jnp.bfloat16),
            in_specs=[pl.BlockSpec(memory_space=pltpu.HBM)] * 9,
            out_specs=pl.BlockSpec(memory_space=pltpu.VMEM),
            scratch_shapes=scratch,
            compiler_params=pltpu.CompilerParams(
                collective_id=0, has_side_effects=True, vmem_limit_bytes=48 * 2**20
            ),
        )(*(pltpu.with_memory_space_constraint(operand, pltpu.HBM) for operand in operands))

    in_specs = (
        P("ctx", "mp"),
        P("ctx", "mp"),
        P("ctx", "mp"),
        P("ctx", None),
        P("ctx", None),
        P(None, "mp"),
        P("mp"),
        P(None, "mp"),
        P("mp"),
    )
    return jax.shard_map(body, mesh=mesh, in_specs=in_specs, out_specs=P("ctx", "mp"), check_vma=False)
```

```python
import functools

import jax
import jax.numpy as jnp
from jax import lax
from jax.experimental import pallas as pl
from jax.experimental.pallas import tpu as pltpu
from jax.sharding import PartitionSpec as P

MESH = pl.DeviceIdType.MESH
F32 = jnp.float32
LANES = 128
SUB = 8
LINE = 8
HEAD = 4
LINE_RANKS = (0, 1, 2, 3, 4, 5, 6, 7)
FAR_FIRST = (4, 3, 5, 2, 6, 1, 7)
BLOCK = 32
SCAN = 42
LOG2E = 1.4426950408889634
LN2 = 0.6931471805599453
SHARES = ((0, 1, 2, 3), (4, 5, 6, 7), (8, 9, 10, 11, 12, 13, 14, 15))


def tile(index, count=1):
    if isinstance(index, int):
        return pl.ds(index * SUB, count * SUB)
    return pl.ds(pl.multiple_of(index * SUB, SUB), count * SUB)


def splat(ref, index):
    return ref[pl.ds(index, SUB, stride=0), :]


def kernel(lines, x_hbm, z_hbm, dt_hbm, b_hbm, c_hbm, w_hbm, bias_hbm, a_hbm, skip_hbm, out_ref,
           x_in, z_in, dt_in, b_in, c_in, w_in, bias_in, a_in, skip_in,
           x_rows, dt_rows, u_rows, y_rows, gate, b_splat, c_splat, rates, taps, decayed,
           halo, parts_out, parts_in, total_out, total_in, carry, spans, starts_out, starts,
           load_sem, dt_sem, x_sem, place_sem, line_sem, halo_sem, send1, recv1, send2, recv2, send3, recv3):
    tokens, channels = x_in.shape
    states = a_in.shape[0]
    per = states // LINE
    groups = channels // LANES
    me = lax.axis_index("ctx")
    line, place = me // LINE, me % LINE
    count = lines * LINE

    pairs = ((b_hbm, b_in), (a_hbm, a_in), (w_hbm, w_in),
             (bias_hbm, bias_in), (skip_hbm, skip_in), (c_hbm, c_in), (z_hbm, z_in))
    loads = [pltpu.make_async_copy(src, dst, load_sem.at[i]) for i, (src, dst) in enumerate(pairs)]
    blocks = tokens // BLOCK

    def chunk(i, src, dst, sem):
        rows = pl.ds(pl.multiple_of(i * BLOCK, BLOCK), BLOCK)
        return pltpu.make_async_copy(src.at[rows], dst.at[rows], sem.at[i])

    def chunks(i):
        return chunk(i, dt_hbm, dt_in, dt_sem), chunk(i, x_hbm, x_in, x_sem)

    for load in loads[:2]:
        load.start()
    for i in range(blocks):
        for load in chunks(i):
            load.start()
    for load in loads[2:]:
        load.start()
    b_load, a_load, w_load, bias_load, skip_load, c_load, z_load = loads

    mp = lax.axis_index("mp")
    late_line, late_column = (mp == 0) & (line == 0), (mp == 0) & (place == 0)

    def place_rank(at):
        rank = jnp.where(at < LINE // 2, at, LINE + LINE // 2 - 1 - at)
        return jnp.where(late_line, jnp.where(at == 0, LINE - 1, rank - 1), rank)

    def line_rank(at):
        rank = 0
        for other, value in enumerate(LINE_RANKS):
            rank = rank + jnp.where(at == other, value, 0)
        return jnp.where(late_column, jnp.where(at == 0, lines - 1, rank - 1), rank)

    my_place_rank, my_line_rank = place_rank(place), line_rank(line)
    barrier = pltpu.get_barrier_semaphore()

    def signal(semaphore, target):
        pl.semaphore_signal(semaphore, inc=1, device_id={"ctx": target}, device_id_type=MESH)

    for step in range(1, LINE):
        target = (place + step) % LINE

        @pl.when(place_rank(target) > my_place_rank)
        def _():
            signal(barrier, line * LINE + target)
    for other in range(lines):
        @pl.when(line_rank(other) > my_line_rank)
        def _():
            signal(barrier, other * LINE + place)

    @pl.when(jnp.where(place == 0, line > 0, place_rank(place - 1) < my_place_rank))
    def _():
        signal(barrier, me - 1)

    def greet():
        after = jnp.where(place == LINE - 1, me < count - 1, place_rank(place + 1) > my_place_rank)
        pl.semaphore_wait(barrier, my_place_rank + my_line_rank + jnp.where(after, 1, 0))
        for step in range(1, LINE):
            target = (place + step) % LINE

            greeted = (place > 0) if step == LINE - 1 else False

            @pl.when((place_rank(target) < my_place_rank) & jnp.logical_not(greeted))
            def _():
                signal(place_sem.at[LINE - step], line * LINE + target)
        for step in range(1, lines):
            @pl.when((line >= step) & (line_rank(line - step) < my_line_rank))
            def _():
                signal(line_sem.at[step], (line - step) * LINE + place)

    def know_place(step):
        known = (place < LINE - 1) if step == 1 else False

        @pl.when((place_rank((place + step) % LINE) > my_place_rank) & jnp.logical_not(known))
        def _():
            pl.semaphore_wait(place_sem.at[step], 1)

    def know_line(step):
        @pl.when(line_rank(line + step) > my_line_rank)
        def _():
            pl.semaphore_wait(line_sem.at[step], 1)

    def copy_to(src, dst, send, recv, target):
        return pltpu.make_async_remote_copy(src_ref=src, dst_ref=dst, send_sem=send, recv_sem=recv,
                                            device_id={"ctx": target}, device_id_type=MESH)

    halo_copy = copy_to(x_rows.at[pl.ds((tokens - 3) * SUB, 3 * SUB)], halo, halo_sem.at[0], halo_sem.at[1], me + 1)

    zero = jnp.zeros((SUB, LANES), F32)
    one = jnp.ones((SUB, LANES), F32)

    def spread(src, dst, scale=None):
        wide = 2 * LANES
        for n in range(0, states, 2):
            state_of = lax.broadcasted_iota(jnp.int32, (states, wide), 0)
            lane = lax.broadcasted_iota(jnp.int32, (states, wide), 1)
            pick = jnp.where(state_of == n + lane // LANES, 1.0, 0.0).astype(jnp.bfloat16)
            both = lax.dot_general(src[...], pick, (((0,), (0,)), ((), ())), preferred_element_type=F32)
            if scale is not None:
                both = both * scale
            dst[n * tokens:(n + 1) * tokens, :] = both[:, :LANES]
            dst[(n + 1) * tokens:(n + 2) * tokens, :] = both[:, LANES:]

    b_load.wait()
    spread(b_in, b_splat)

    a_load.wait()
    for j in range(groups):
        rates[pl.ds(j, states, stride=SUB), :] = -jnp.exp(a_in[:, j * LANES:(j + 1) * LANES])

    soon = ((place >= LINE // 2) & (place < LINE - 1)) | (late_line & (place == 0))
    pl.when(soon)(greet)
    def lay_out(i):
        for load in chunks(i):
            load.wait()
        rows = pl.ds(pl.multiple_of(i * BLOCK, BLOCK), BLOCK)
        for j in range(groups):
            at = pl.ds(i * BLOCK * SUB + j, BLOCK, stride=SUB)
            raw = dt_in[rows, j * LANES:(j + 1) * LANES].astype(F32)
            dt_rows[at, :] = jnp.log2(1.0 + jnp.exp2(raw * LOG2E))
            x_rows[at, :] = x_in[rows, j * LANES:(j + 1) * LANES].astype(F32)

    lay_out(jnp.int32(0))
    w_load.wait()
    bias_load.wait()
    skip_load.wait()
    for j in range(groups):
        taps[pl.ds(j, 4, stride=SUB), :] = 0.5 * w_in[:, j * LANES:(j + 1) * LANES]
    tap = [taps[tile(k), :] for k in range(4)]
    bias = 0.5 * bias_in[...]

    def mix_token(t, window):
        half = bias + tap[0] * window[0] + tap[1] * window[1] + tap[2] * window[2] + tap[3] * window[3]
        inner = half + half * jnp.tanh(half)
        u_rows[tile(t), :] = dt_rows[tile(t), :] * inner
        y_rows[tile(t), :] = inner

    def mix_block(i, carried):
        x0, x1, x2, total = carried
        for k in range(BLOCK):
            t = i * BLOCK + k
            x3 = x_rows[tile(t), :]
            mix_token(t, (x0, x1, x2, x3))
            total = total + dt_rows[tile(t), :]
            x0, x1, x2 = x1, x2, x3
        return x0, x1, x2, total

    def mix(i, carried):
        lay_out(i + 1)
        return mix_block(i, carried)

    carried = lax.fori_loop(0, blocks - 1, mix, (zero,) * 4)
    pl.when(jnp.logical_not(soon))(greet)

    @pl.when(me < count - 1)
    def _():
        halo_copy.start()

    *_, total = mix_block(jnp.int32(blocks - 1), carried)
    head_total = zero
    for t in range(HEAD):
        head_total = head_total + dt_rows[tile(t), :]

    def advance(group, t, state):
        step = dt_rows[tile(t), :]
        drive = u_rows[tile(t), :]
        return tuple(jnp.exp2(rates[tile(n), :] * step) * now + drive * splat(b_splat, n * tokens + t)
                     for n, now in zip(group, state))

    def local_end(group):
        def some(i, state):
            for k in range(SCAN):
                state = advance(group, HEAD + i * SCAN + k, state)
            return state
        return lax.fori_loop(0, (tokens - HEAD) // SCAN, some, (zero,) * len(group))

    halves = (range(states // 2), range(states // 2, states))
    state = local_end(halves[0])

    state = state + local_end(halves[1])

    @pl.when(me > 0)
    def _():
        halo_copy.wait_recv()

    @pl.when(me == 0)
    def _():
        halo[...] = jnp.zeros((3 * SUB, LANES), F32)

    window = [halo[tile(t), :] for t in range(3)] + [x_rows[tile(t), :] for t in range(HEAD)]
    for t in range(HEAD):
        mix_token(t, window[t:t + 4])
    early = (zero,) * states
    for t in range(HEAD):
        early = advance(range(states), t, early)
    rest = total - head_total
    for n in range(states):
        owner, slot = n // per, n % per
        parts_out[tile(owner * (per + 1) + slot), :] = state[n] + jnp.exp2(rates[tile(n), :] * rest) * early[n]
    for owner in range(LINE):
        parts_out[tile(owner * (per + 1) + per), :] = total

    size = (per + 1) * SUB
    mine = pl.ds(pl.multiple_of(place * size, SUB), size)
    sent = []
    for step in FAR_FIRST:
        know_place(step)
        target = (place + step) % LINE
        theirs = pl.ds(pl.multiple_of(target * size, SUB), size)
        copy = copy_to(parts_out.at[theirs], parts_in.at[mine], send1.at[step], recv1.at[step], line * LINE + target)
        copy.start()
        sent.append(copy)
    parts_in[mine, :] = parts_out[mine, :]

    skip = skip_in[...]

    def read_out(mine_states):
        steps = 64 // len(mine_states)

        def some(i, carried):
            states_now, decays = carried
            for k in range(steps):
                t = i * steps + k
                step = dt_rows[tile(t), :]
                drive = u_rows[tile(t), :]
                y = y_rows[tile(t), :]
                if 0 in mine_states:
                    y = skip * y
                states_next, decays_next = [], []
                for m, n in enumerate(mine_states):
                    decay = jnp.exp2(rates[tile(n), :] * step)
                    read = splat(c_splat, n * tokens + t)
                    now = decay * states_now[m] + drive * splat(b_splat, n * tokens + t)
                    since = decay * decays[m]
                    y = y + read * now
                    decayed[tile(t * states + n), :] = read * since
                    states_next.append(now)
                    decays_next.append(since)
                y_rows[tile(t), :] = y
                states_now, decays = tuple(states_next), tuple(decays_next)
            return states_now, decays
        size = len(mine_states)
        lax.fori_loop(0, tokens // steps, some, ((zero,) * size, (one,) * size))

    c_load.wait()
    spread(c_in, c_splat, LN2)
    read_out(SHARES[0])
    for copy in sent:
        copy.wait_recv()
    own_rate = [rates[tile(place * per + m), :] for m in range(per)]
    ahead = [zero] * per
    span = zero
    for other in range(LINE):
        step = parts_in[tile(other * (per + 1) + per), :]
        for m in range(per):
            starts_out[tile(other * per + m), :] = ahead[m]
            spans[tile(other * per + m), :] = jnp.exp2(own_rate[m] * span)
            ahead[m] = jnp.exp2(own_rate[m] * step) * ahead[m] + parts_in[tile(other * (per + 1) + m), :]
        span = span + step
    for m in range(per):
        total_out[tile(m), :] = ahead[m]
    total_out[tile(per), :] = span

    my_line = pl.ds(pl.multiple_of(line * size, SUB), size)

    def line_copy(step):
        return copy_to(total_out, total_in.at[my_line], send2.at[step], recv2.at[step], (line + step) * LINE + place)

    for step in range(1, lines):
        @pl.when(line + step < lines)
        def _():
            know_line(step)
            line_copy(step).start()


    z_load.wait()

    def gates(i, _):
        rows = pl.ds(pl.multiple_of(i * 16, 16), 16)
        for j in range(groups):
            half = 0.5 * z_in[rows, j * LANES:(j + 1) * LANES].astype(F32)
            gate[rows, j * LANES:(j + 1) * LANES] = half + half * jnp.tanh(half)
        return 0

    lax.fori_loop(0, tokens // 16, gates, 0)

    read_out(SHARES[1])

    for m in range(per):
        carry[tile(m), :] = zero
    for step in range(lines - 1, 0, -1):
        @pl.when(line >= step)
        def _():
            line_copy(step).wait_recv()
            first = (line - step) * (per + 1)
            step_sum = total_in[tile(first + per), :]
            for m in range(per):
                decay = jnp.exp2(own_rate[m] * step_sum)
                carry[tile(m), :] = decay * carry[tile(m), :] + total_in[tile(first + m), :]

    for other in range(LINE):
        for m in range(per):
            at = tile(other * per + m)
            starts_out[at, :] = starts_out[at, :] + spans[at, :] * carry[tile(m), :]
    mine = tile(place * per, per)

    def start_copy(step):
        target = (place + step) % LINE
        return copy_to(starts_out.at[tile(target * per, per)], starts.at[mine], send3.at[step], recv3.at[step],
                       line * LINE + target)

    returned = [start_copy(step) for step in range(1, LINE)]
    for target in (0, 1, 2, 3, 7, 6, 5, 4):
        @pl.when(place != target)
        def _():
            start_copy((target + LINE - place) % LINE).start()
    starts[mine, :] = starts_out[mine, :]

    read_out(SHARES[2])

    def start_terms(owners, t):
        terms = []
        for first, start in owners:
            for m in range(per):
                terms.append(decayed[tile(t * states + first + m), :] * start[m])
        return terms

    def tree(terms):
        while len(terms) > 1:
            terms = [terms[q] + terms[q + 1] if q + 1 < len(terms) else terms[q] for q in range(0, len(terms), 2)]
        return terms[0]

    def arrived(steps):
        owners = []
        for step in steps:
            if step:
                returned[step - 1].wait_recv()
            first = ((place + LINE - step) % LINE) * per
            owners.append((first, [starts[tile(first + m), :] for m in range(per)]))
        return owners

    for steps in ((0, 1, LINE - 1), (2, LINE - 2), (3, LINE - 3)):
        owners = arrived(steps)

        def add(i, _):
            for k in range(16):
                t = i * 16 + k
                y_rows[tile(t), :] = tree(start_terms(owners, t) + [y_rows[tile(t), :]])
            return 0

        lax.fori_loop(0, tokens // 16, add, 0)
    far = arrived((LINE // 2,))

    def finish(i, _):
        for k in range(16):
            t = i * 16 + k
            y_rows[tile(t), :] = tree(start_terms(far, t) + [y_rows[tile(t), :]])
        rows = pl.ds(pl.multiple_of(i * 16, 16), 16)
        for j in range(groups):
            mixed = y_rows[pl.ds(i * 16 * SUB + j, 16, stride=SUB), :]
            at = slice(j * LANES, (j + 1) * LANES)
            out_ref[rows, at] = (mixed * gate[rows, at]).astype(jnp.bfloat16)
        return 0

    lax.fori_loop(0, tokens // 16, finish, 0)

    @pl.when(me < count - 1)
    def _():
        halo_copy.wait_send()

    for copy in sent + returned:
        copy.wait_send()
    for step in range(1, lines):
        @pl.when(line + step < lines)
        def _():
            line_copy(step).wait_send()


def solution(mesh):
    count = mesh.shape["ctx"]
    lines = count // LINE

    def body(x_in, z_gate, dt_raw, b_proj, c_proj, conv_weight, conv_bias, a_log, d_skip):
        tokens, channels = x_in.shape
        states = a_log.shape[0]
        per = states // LINE
        groups = channels // LANES

        def block(*shape, dtype=F32):
            return pltpu.VMEM(shape, dtype)

        def rows(number):
            return block(number * SUB, LANES)

        bf16 = functools.partial(block, dtype=jnp.bfloat16)
        scratch = [
            bf16(tokens, channels), bf16(tokens, channels), bf16(tokens, channels), bf16(states, tokens), bf16(states, tokens),
            block(4, channels), block(SUB, LANES), block(states, channels), block(SUB, LANES),
            rows(tokens), rows(tokens), rows(tokens), rows(tokens), block(tokens, channels),
            block(states * tokens + SUB, LANES), block(states * tokens + SUB, LANES), rows(states), rows(4),
            rows(states * tokens),
            rows(3), rows(LINE * (per + 1)), rows(LINE * (per + 1)), rows(per + 1), rows(lines * (per + 1)), rows(per),
            rows(states), rows(states), rows(states),
            pltpu.SemaphoreType.DMA((7,)), pltpu.SemaphoreType.DMA((tokens // BLOCK,)), pltpu.SemaphoreType.DMA((tokens // BLOCK,)), pltpu.SemaphoreType.REGULAR((LINE,)),
            pltpu.SemaphoreType.REGULAR((lines,)), pltpu.SemaphoreType.DMA((2,)),
            pltpu.SemaphoreType.DMA((LINE,)), pltpu.SemaphoreType.DMA((LINE,)),
            pltpu.SemaphoreType.DMA((lines,)), pltpu.SemaphoreType.DMA((lines,)),
            pltpu.SemaphoreType.DMA((LINE,)), pltpu.SemaphoreType.DMA((LINE,)),
        ]
        operands = (x_in, z_gate, dt_raw, b_proj.T, c_proj.T, conv_weight, conv_bias.reshape(groups, LANES), a_log,
                    d_skip.reshape(groups, LANES))
        return pl.pallas_call(
            functools.partial(kernel, lines),
            out_shape=pltpu.VMEM((tokens, channels), jnp.bfloat16),
            in_specs=[pl.BlockSpec(memory_space=pltpu.HBM)] * 9,
            out_specs=pl.BlockSpec(memory_space=pltpu.VMEM),
            scratch_shapes=scratch,
            compiler_params=pltpu.CompilerParams(
                collective_id=0, has_side_effects=True, vmem_limit_bytes=48 * 2**20
            ),
        )(*(pltpu.with_memory_space_constraint(operand, pltpu.HBM) for operand in operands))

    in_specs = (
        P("ctx", "mp"),
        P("ctx", "mp"),
        P("ctx", "mp"),
        P("ctx", None),
        P("ctx", None),
        P(None, "mp"),
        P("mp"),
        P(None, "mp"),
        P("mp"),
    )
    return jax.shard_map(body, mesh=mesh, in_specs=in_specs, out_specs=P("ctx", "mp"), check_vma=False)
```

```python
import functools

import jax
import jax.numpy as jnp
from jax import lax
from jax.experimental import pallas as pl
from jax.experimental.pallas import tpu as pltpu
from jax.sharding import PartitionSpec as P

MESH = pl.DeviceIdType.MESH
F32 = jnp.float32
LANES = 128
SUB = 8
LINE = 8
HEAD = 4
LINE_RANKS = (0, 1, 2, 3, 4, 5, 6, 7)
FAR_FIRST = (4, 3, 5, 2, 6, 1, 7)
BLOCK = 32
SCAN = 42
LOG2E = 1.4426950408889634
LN2 = 0.6931471805599453
SHARES = (((0, 1, 2, 3), (4, 5)), ((6, 7, 8, 9), (10, 11)), ((12, 13, 14, 15),))


def tile(index, count=1):
    if isinstance(index, int):
        return pl.ds(index * SUB, count * SUB)
    return pl.ds(pl.multiple_of(index * SUB, SUB), count * SUB)


def splat(ref, index):
    return ref[pl.ds(index, SUB, stride=0), :]


def kernel(lines, x_hbm, z_hbm, dt_hbm, b_hbm, c_hbm, w_hbm, bias_hbm, a_hbm, skip_hbm, out_ref,
           x_in, z_in, dt_in, b_in, c_in, w_in, bias_in, a_in, skip_in,
           x_rows, dt_rows, u_rows, y_rows, gate, b_splat, c_splat, rates, taps, decayed,
           halo, parts_out, parts_in, total_out, total_in, carry, spans, starts_out, starts,
           load_sem, dt_sem, x_sem, place_sem, line_sem, halo_sem, send1, recv1, send2, recv2, send3, recv3):
    tokens, channels = x_in.shape
    states = a_in.shape[0]
    per = states // LINE
    groups = channels // LANES
    me = lax.axis_index("ctx")
    line, place = me // LINE, me % LINE
    count = lines * LINE

    pairs = ((b_hbm, b_in), (a_hbm, a_in), (w_hbm, w_in),
             (bias_hbm, bias_in), (skip_hbm, skip_in), (c_hbm, c_in), (z_hbm, z_in))
    loads = [pltpu.make_async_copy(src, dst, load_sem.at[i]) for i, (src, dst) in enumerate(pairs)]
    blocks = tokens // BLOCK

    def chunk(i, src, dst, sem):
        rows = pl.ds(pl.multiple_of(i * BLOCK, BLOCK), BLOCK)
        return pltpu.make_async_copy(src.at[rows], dst.at[rows], sem.at[i])

    def chunks(i):
        return chunk(i, dt_hbm, dt_in, dt_sem), chunk(i, x_hbm, x_in, x_sem)

    for load in loads[:2]:
        load.start()
    for i in range(blocks):
        for load in chunks(i):
            load.start()
    for load in loads[2:]:
        load.start()
    b_load, a_load, w_load, bias_load, skip_load, c_load, z_load = loads

    mp = lax.axis_index("mp")
    late_line, late_column = (mp == 0) & (line == 0), (mp == 0) & (place == 0)

    def place_rank(at):
        rank = jnp.where(at < LINE // 2, at, LINE + LINE // 2 - 1 - at)
        return jnp.where(late_line, jnp.where(at == 0, LINE - 1, rank - 1), rank)

    def line_rank(at):
        rank = 0
        for other, value in enumerate(LINE_RANKS):
            rank = rank + jnp.where(at == other, value, 0)
        return jnp.where(late_column, jnp.where(at == 0, lines - 1, rank - 1), rank)

    my_place_rank, my_line_rank = place_rank(place), line_rank(line)
    barrier = pltpu.get_barrier_semaphore()

    def signal(semaphore, target):
        pl.semaphore_signal(semaphore, inc=1, device_id={"ctx": target}, device_id_type=MESH)

    for step in range(1, LINE):
        target = (place + step) % LINE

        @pl.when(place_rank(target) > my_place_rank)
        def _():
            signal(barrier, line * LINE + target)
    for other in range(lines):
        @pl.when(line_rank(other) > my_line_rank)
        def _():
            signal(barrier, other * LINE + place)

    @pl.when(jnp.where(place == 0, line > 0, place_rank(place - 1) < my_place_rank))
    def _():
        signal(barrier, me - 1)

    def greet():
        after = jnp.where(place == LINE - 1, me < count - 1, place_rank(place + 1) > my_place_rank)
        pl.semaphore_wait(barrier, my_place_rank + my_line_rank + jnp.where(after, 1, 0))
        for step in range(1, LINE):
            target = (place + step) % LINE

            greeted = (place > 0) if step == LINE - 1 else False

            @pl.when((place_rank(target) < my_place_rank) & jnp.logical_not(greeted))
            def _():
                signal(place_sem.at[LINE - step], line * LINE + target)
        for step in range(1, lines):
            @pl.when((line >= step) & (line_rank(line - step) < my_line_rank))
            def _():
                signal(line_sem.at[step], (line - step) * LINE + place)

    def know_place(step):
        known = (place < LINE - 1) if step == 1 else False

        @pl.when((place_rank((place + step) % LINE) > my_place_rank) & jnp.logical_not(known))
        def _():
            pl.semaphore_wait(place_sem.at[step], 1)

    def know_line(step):
        @pl.when(line_rank(line + step) > my_line_rank)
        def _():
            pl.semaphore_wait(line_sem.at[step], 1)

    def copy_to(src, dst, send, recv, target):
        return pltpu.make_async_remote_copy(src_ref=src, dst_ref=dst, send_sem=send, recv_sem=recv,
                                            device_id={"ctx": target}, device_id_type=MESH)

    halo_copy = copy_to(x_rows.at[pl.ds((tokens - 3) * SUB, 3 * SUB)], halo, halo_sem.at[0], halo_sem.at[1], me + 1)

    zero = jnp.zeros((SUB, LANES), F32)
    one = jnp.ones((SUB, LANES), F32)

    def spread(src, dst, scale=None):
        wide = 2 * LANES
        for n in range(0, states, 2):
            state_of = lax.broadcasted_iota(jnp.int32, (states, wide), 0)
            lane = lax.broadcasted_iota(jnp.int32, (states, wide), 1)
            pick = jnp.where(state_of == n + lane // LANES, 1.0, 0.0).astype(jnp.bfloat16)
            both = lax.dot_general(src[...], pick, (((0,), (0,)), ((), ())), preferred_element_type=F32)
            if scale is not None:
                both = both * scale
            dst[n * tokens:(n + 1) * tokens, :] = both[:, :LANES]
            dst[(n + 1) * tokens:(n + 2) * tokens, :] = both[:, LANES:]

    b_load.wait()
    spread(b_in, b_splat)

    a_load.wait()
    for j in range(groups):
        rates[pl.ds(j, states, stride=SUB), :] = -jnp.exp(a_in[:, j * LANES:(j + 1) * LANES])

    soon = ((place >= LINE // 2) & (place < LINE - 1)) | (late_line & (place == 0))
    pl.when(soon)(greet)
    def lay_out(i):
        for load in chunks(i):
            load.wait()
        rows = pl.ds(pl.multiple_of(i * BLOCK, BLOCK), BLOCK)
        for j in range(groups):
            at = pl.ds(i * BLOCK * SUB + j, BLOCK, stride=SUB)
            raw = dt_in[rows, j * LANES:(j + 1) * LANES].astype(F32)
            dt_rows[at, :] = jnp.log2(1.0 + jnp.exp2(raw * LOG2E))
            x_rows[at, :] = x_in[rows, j * LANES:(j + 1) * LANES].astype(F32)

    lay_out(jnp.int32(0))
    w_load.wait()
    bias_load.wait()
    skip_load.wait()
    for j in range(groups):
        taps[pl.ds(j, 4, stride=SUB), :] = 0.5 * w_in[:, j * LANES:(j + 1) * LANES]
    tap = [taps[tile(k), :] for k in range(4)]
    bias = 0.5 * bias_in[...]

    def mix_token(t, window):
        half = bias + tap[0] * window[0] + tap[1] * window[1] + tap[2] * window[2] + tap[3] * window[3]
        inner = half + half * jnp.tanh(half)
        u_rows[tile(t), :] = dt_rows[tile(t), :] * inner
        y_rows[tile(t), :] = inner

    def mix_block(i, carried):
        x0, x1, x2, total = carried
        for k in range(BLOCK):
            t = i * BLOCK + k
            x3 = x_rows[tile(t), :]
            mix_token(t, (x0, x1, x2, x3))
            total = total + dt_rows[tile(t), :]
            x0, x1, x2 = x1, x2, x3
        return x0, x1, x2, total

    def mix(i, carried):
        lay_out(i + 1)
        return mix_block(i, carried)

    carried = lax.fori_loop(0, blocks - 1, mix, (zero,) * 4)
    pl.when(jnp.logical_not(soon))(greet)

    @pl.when(me < count - 1)
    def _():
        halo_copy.start()

    *_, total = mix_block(jnp.int32(blocks - 1), carried)
    head_total = zero
    for t in range(HEAD):
        head_total = head_total + dt_rows[tile(t), :]

    def advance(group, t, state):
        step = dt_rows[tile(t), :]
        drive = u_rows[tile(t), :]
        return tuple(jnp.exp2(rates[tile(n), :] * step) * now + drive * splat(b_splat, n * tokens + t)
                     for n, now in zip(group, state))

    def local_end(group):
        def some(i, state):
            for k in range(SCAN):
                state = advance(group, HEAD + i * SCAN + k, state)
            return state
        return lax.fori_loop(0, (tokens - HEAD) // SCAN, some, (zero,) * len(group))

    halves = (range(states // 2), range(states // 2, states))
    state = local_end(halves[0])

    state = state + local_end(halves[1])

    @pl.when(me > 0)
    def _():
        halo_copy.wait_recv()

    @pl.when(me == 0)
    def _():
        halo[...] = jnp.zeros((3 * SUB, LANES), F32)

    window = [halo[tile(t), :] for t in range(3)] + [x_rows[tile(t), :] for t in range(HEAD)]
    for t in range(HEAD):
        mix_token(t, window[t:t + 4])
    early = (zero,) * states
    for t in range(HEAD):
        early = advance(range(states), t, early)
    rest = total - head_total
    for n in range(states):
        owner, slot = n // per, n % per
        parts_out[tile(owner * (per + 1) + slot), :] = state[n] + jnp.exp2(rates[tile(n), :] * rest) * early[n]
    for owner in range(LINE):
        parts_out[tile(owner * (per + 1) + per), :] = total

    size = (per + 1) * SUB
    mine = pl.ds(pl.multiple_of(place * size, SUB), size)
    sent = []
    for step in FAR_FIRST:
        know_place(step)
        target = (place + step) % LINE
        theirs = pl.ds(pl.multiple_of(target * size, SUB), size)
        copy = copy_to(parts_out.at[theirs], parts_in.at[mine], send1.at[step], recv1.at[step], line * LINE + target)
        copy.start()
        sent.append(copy)
    parts_in[mine, :] = parts_out[mine, :]

    skip = skip_in[...]

    def read_out(mine_states):
        steps = 64 // len(mine_states)

        def some(i, carried):
            states_now, decays = carried
            for k in range(steps):
                t = i * steps + k
                step = dt_rows[tile(t), :]
                drive = u_rows[tile(t), :]
                y = y_rows[tile(t), :]
                if 0 in mine_states:
                    y = skip * y
                states_next, decays_next = [], []
                for m, n in enumerate(mine_states):
                    decay = jnp.exp2(rates[tile(n), :] * step)
                    read = splat(c_splat, n * tokens + t)
                    now = decay * states_now[m] + drive * splat(b_splat, n * tokens + t)
                    since = decay * decays[m]
                    y = y + read * now
                    decayed[tile(t * states + n), :] = read * since
                    states_next.append(now)
                    decays_next.append(since)
                y_rows[tile(t), :] = y
                states_now, decays = tuple(states_next), tuple(decays_next)
            return states_now, decays
        size = len(mine_states)
        lax.fori_loop(0, tokens // steps, some, ((zero,) * size, (one,) * size))

    c_load.wait()
    spread(c_in, c_splat, LN2)
    for share in SHARES[0]:
        read_out(share)
    for copy in sent:
        copy.wait_recv()
    own_rate = [rates[tile(place * per + m), :] for m in range(per)]
    ahead = [zero] * per
    span = zero
    for other in range(LINE):
        step = parts_in[tile(other * (per + 1) + per), :]
        for m in range(per):
            starts_out[tile(other * per + m), :] = ahead[m]
            spans[tile(other * per + m), :] = jnp.exp2(own_rate[m] * span)
            ahead[m] = jnp.exp2(own_rate[m] * step) * ahead[m] + parts_in[tile(other * (per + 1) + m), :]
        span = span + step
    for m in range(per):
        total_out[tile(m), :] = ahead[m]
    total_out[tile(per), :] = span

    my_line = pl.ds(pl.multiple_of(line * size, SUB), size)

    def line_copy(step):
        return copy_to(total_out, total_in.at[my_line], send2.at[step], recv2.at[step], (line + step) * LINE + place)

    for step in range(1, lines):
        @pl.when(line + step < lines)
        def _():
            know_line(step)
            line_copy(step).start()


    z_load.wait()

    def gates(i, _):
        rows = pl.ds(pl.multiple_of(i * 16, 16), 16)
        for j in range(groups):
            half = 0.5 * z_in[rows, j * LANES:(j + 1) * LANES].astype(F32)
            gate[rows, j * LANES:(j + 1) * LANES] = half + half * jnp.tanh(half)
        return 0

    lax.fori_loop(0, tokens // 16, gates, 0)

    for share in SHARES[1]:
        read_out(share)

    for m in range(per):
        carry[tile(m), :] = zero
    for step in range(lines - 1, 0, -1):
        @pl.when(line >= step)
        def _():
            line_copy(step).wait_recv()
            first = (line - step) * (per + 1)
            step_sum = total_in[tile(first + per), :]
            for m in range(per):
                decay = jnp.exp2(own_rate[m] * step_sum)
                carry[tile(m), :] = decay * carry[tile(m), :] + total_in[tile(first + m), :]

    for other in range(LINE):
        for m in range(per):
            at = tile(other * per + m)
            starts_out[at, :] = starts_out[at, :] + spans[at, :] * carry[tile(m), :]
    mine = tile(place * per, per)

    def start_copy(step):
        target = (place + step) % LINE
        return copy_to(starts_out.at[tile(target * per, per)], starts.at[mine], send3.at[step], recv3.at[step],
                       line * LINE + target)

    returned = [start_copy(step) for step in range(1, LINE)]
    for target in (0, 1, 2, 3, 7, 6, 5, 4):
        @pl.when(place != target)
        def _():
            start_copy((target + LINE - place) % LINE).start()
    starts[mine, :] = starts_out[mine, :]

    for share in SHARES[2]:
        read_out(share)

    def start_terms(owners, t):
        terms = []
        for first, start in owners:
            for m in range(per):
                terms.append(decayed[tile(t * states + first + m), :] * start[m])
        return terms

    def tree(terms):
        while len(terms) > 1:
            terms = [terms[q] + terms[q + 1] if q + 1 < len(terms) else terms[q] for q in range(0, len(terms), 2)]
        return terms[0]

    def arrived(steps):
        owners = []
        for step in steps:
            if step:
                returned[step - 1].wait_recv()
            first = ((place + LINE - step) % LINE) * per
            owners.append((first, [starts[tile(first + m), :] for m in range(per)]))
        return owners

    for steps in ((0, 1, LINE - 1), (2, LINE - 2), (3, LINE - 3)):
        owners = arrived(steps)

        def add(i, _):
            for k in range(16):
                t = i * 16 + k
                y_rows[tile(t), :] = tree(start_terms(owners, t) + [y_rows[tile(t), :]])
            return 0

        lax.fori_loop(0, tokens // 16, add, 0)
    far = arrived((LINE // 2,))

    def finish(i, _):
        for k in range(16):
            t = i * 16 + k
            y_rows[tile(t), :] = tree(start_terms(far, t) + [y_rows[tile(t), :]])
        rows = pl.ds(pl.multiple_of(i * 16, 16), 16)
        for j in range(groups):
            mixed = y_rows[pl.ds(i * 16 * SUB + j, 16, stride=SUB), :]
            at = slice(j * LANES, (j + 1) * LANES)
            out_ref[rows, at] = (mixed * gate[rows, at]).astype(jnp.bfloat16)
        return 0

    lax.fori_loop(0, tokens // 16, finish, 0)

    @pl.when(me < count - 1)
    def _():
        halo_copy.wait_send()

    for copy in sent + returned:
        copy.wait_send()
    for step in range(1, lines):
        @pl.when(line + step < lines)
        def _():
            line_copy(step).wait_send()


def solution(mesh):
    count = mesh.shape["ctx"]
    lines = count // LINE

    def body(x_in, z_gate, dt_raw, b_proj, c_proj, conv_weight, conv_bias, a_log, d_skip):
        tokens, channels = x_in.shape
        states = a_log.shape[0]
        per = states // LINE
        groups = channels // LANES

        def block(*shape, dtype=F32):
            return pltpu.VMEM(shape, dtype)

        def rows(number):
            return block(number * SUB, LANES)

        bf16 = functools.partial(block, dtype=jnp.bfloat16)
        scratch = [
            bf16(tokens, channels), bf16(tokens, channels), bf16(tokens, channels), bf16(states, tokens), bf16(states, tokens),
            block(4, channels), block(SUB, LANES), block(states, channels), block(SUB, LANES),
            rows(tokens), rows(tokens), rows(tokens), rows(tokens), block(tokens, channels),
            block(states * tokens + SUB, LANES), block(states * tokens + SUB, LANES), rows(states), rows(4),
            rows(states * tokens),
            rows(3), rows(LINE * (per + 1)), rows(LINE * (per + 1)), rows(per + 1), rows(lines * (per + 1)), rows(per),
            rows(states), rows(states), rows(states),
            pltpu.SemaphoreType.DMA((7,)), pltpu.SemaphoreType.DMA((tokens // BLOCK,)), pltpu.SemaphoreType.DMA((tokens // BLOCK,)), pltpu.SemaphoreType.REGULAR((LINE,)),
            pltpu.SemaphoreType.REGULAR((lines,)), pltpu.SemaphoreType.DMA((2,)),
            pltpu.SemaphoreType.DMA((LINE,)), pltpu.SemaphoreType.DMA((LINE,)),
            pltpu.SemaphoreType.DMA((lines,)), pltpu.SemaphoreType.DMA((lines,)),
            pltpu.SemaphoreType.DMA((LINE,)), pltpu.SemaphoreType.DMA((LINE,)),
        ]
        operands = (x_in, z_gate, dt_raw, b_proj.T, c_proj.T, conv_weight, conv_bias.reshape(groups, LANES), a_log,
                    d_skip.reshape(groups, LANES))
        return pl.pallas_call(
            functools.partial(kernel, lines),
            out_shape=pltpu.VMEM((tokens, channels), jnp.bfloat16),
            in_specs=[pl.BlockSpec(memory_space=pltpu.HBM)] * 9,
            out_specs=pl.BlockSpec(memory_space=pltpu.VMEM),
            scratch_shapes=scratch,
            compiler_params=pltpu.CompilerParams(
                collective_id=0, has_side_effects=True, vmem_limit_bytes=48 * 2**20
            ),
        )(*(pltpu.with_memory_space_constraint(operand, pltpu.HBM) for operand in operands))

    in_specs = (
        P("ctx", "mp"),
        P("ctx", "mp"),
        P("ctx", "mp"),
        P("ctx", None),
        P("ctx", None),
        P(None, "mp"),
        P("mp"),
        P(None, "mp"),
        P("mp"),
    )
    return jax.shard_map(body, mesh=mesh, in_specs=in_specs, out_specs=P("ctx", "mp"), check_vma=False)
```
